32 devices in a mesh: dp: 8 (over z, y), mp: 4 (over x, core).
Axes of the slice: x: 2, y: 2, z: 4, core: 2. Of those that a mesh axis runs over, the one named last changes fastest.
Arguments:
- inputs: bfloat16 [8, 512, 4096], P('dp', None, 'mp'), may hold values from -6 to 6
- out_grads: bfloat16 [8, 512, 4096], P('dp', None, 'mp'), may hold values from -6 to 6
- gate_weight: bfloat16 [4096, 14336], P('dp', 'mp'), may hold values from -0.09375 to 0.09375
- down_weight: bfloat16 [14336, 4096], P('mp', 'dp'), may hold values from -0.046875 to 0.046875
- in_proj: bfloat16 [4096, 64], replicated, may hold values from -0.09375 to 0.09375
- out_proj: bfloat16 [14336, 64], P('mp'), may hold values from -0.046875 to 0.046875
- in_precond: float32 [64, 64], replicated, may hold values from -0.75 to 0.75
- out_precond: float32 [64, 64], replicated, may hold values from -0.75 to 0.75
- queries: bfloat16 [1024, 4096], P('dp', 'mp'), may hold values from -48 to 48
- languages: int32 [1024], P('dp'), may hold values from 0 to 31, as said below
Outputs:
- influence: float32 [8, 32], P('dp')
The draws below stay inside these ranges and needn't reach their ends.
Inputs may be any that keep to these rules, and one draw needn't show every extreme that they name: Each of the 32 languages labels exactly 32 queries.
All inputs are finite; a program needn't handle non-finite values.
Results may differ from the reference program's by a relative error of at most 0.0042.
Values may be sent and summed in bfloat16 or wider, within the bound.
A program may use at most 128 MiB of HBM per device.

```python
import jax
import jax.numpy as jnp
from jax import lax

D = 4096
FF = 14336
R = 64
SEQ = 512
LANGS = 32
EXAMPLES = 8
QUERIES = 1024


def draw_languages(key, part):
    order = jax.random.permutation(key, QUERIES)
    return (order % LANGS).astype(jnp.int32)


def shard_levels(rng, extent, cuts, smallest, high):
    def one(axis_at, parts):
        heights = jax.random.uniform(jax.random.fold_in(jax.random.fold_in(rng, 6), axis_at), (parts,), jnp.float32, smallest / len(cuts), high / len(cuts))
        return jnp.repeat(jnp.exp(heights), extent[axis_at] // parts).reshape((-1,) + (1,) * (len(extent) - axis_at - 1))

    loudness = one(*cuts[0])
    for cut in cuts[1:]:
        loudness = loudness * one(*cut)
    return loudness


def normal_values(stream_key, shape, scale, limit, pieces=(), held_as=jnp.bfloat16):
    level = shard_levels(stream_key, shape, pieces, -0.22, 0.18) if pieces else 1.0
    result = jax.random.normal(stream_key, shape, jnp.float32) * scale * level
    return jnp.minimum(jnp.maximum(result, -limit), limit).astype(held_as)


def setup_inputs(seed: int = 0) -> dict:
    key_of = jax.random.split(jax.random.key(seed), 11)
    return {
        "inputs": normal_values(key_of[0], (EXAMPLES, SEQ, D), 1.0, 6.0, ((0, 8), (2, 4))),
        "out_grads": normal_values(key_of[1], (EXAMPLES, SEQ, D), 1.0, 6.0, ((0, 8), (2, 4))),
        "gate_weight": normal_values(key_of[2], (D, FF), D ** -0.5, 0.09375, ((0, 8), (1, 4))),
        "down_weight": normal_values(key_of[3], (FF, D), FF ** -0.5, 0.046875, ((0, 4), (1, 8))),
        "in_proj": normal_values(key_of[4], (D, R), D ** -0.5, 0.09375),
        "out_proj": normal_values(key_of[5], (FF, R), FF ** -0.5, 0.046875, ((0, 4),)),
        "in_precond": normal_values(key_of[6], (R, R), R ** -0.5, 0.75, (), jnp.float32),
        "out_precond": normal_values(key_of[7], (R, R), R ** -0.5, 0.75, (), jnp.float32),
        "queries": normal_values(key_of[8], (QUERIES, R * R), 8.0, 48.0, ((0, 8), (1, 4))),
        "languages": draw_languages(jax.random.fold_in(key_of[10], 71), 0),
    }


def reference(inputs, out_grads, gate_weight, down_weight, in_proj, out_proj, in_precond, out_precond, queries, languages):
    def one_example(pair):
        rows, grads = pair
        gate = jnp.dot(rows, gate_weight, preferred_element_type=jnp.float32)
        hidden_grad = jnp.dot(grads, down_weight.T, preferred_element_type=jnp.float32)
        up_grad = (hidden_grad * jax.nn.silu(gate)).astype(jnp.bfloat16)
        in_factor = jnp.dot(jnp.dot(rows, in_proj, preferred_element_type=jnp.float32), in_precond.T, precision=lax.Precision.HIGHEST)
        out_factor = jnp.dot(jnp.dot(up_grad, out_proj, preferred_element_type=jnp.float32), out_precond, precision=lax.Precision.HIGHEST)
        full = jnp.dot(in_factor.T, out_factor, precision=lax.Precision.HIGHEST) / SEQ
        return full.reshape(R * R).astype(jnp.bfloat16)

    projected = lax.map(one_example, (inputs, out_grads))
    scores = jnp.dot(projected, queries.T, preferred_element_type=jnp.float32)
    onehot = (languages[:, None] == jnp.arange(LANGS, dtype=jnp.int32)[None, :]).astype(jnp.float32)
    summed = jnp.dot(scores, onehot, precision=lax.Precision.HIGHEST)
    return summed / (QUERIES // LANGS)
```

```python
import functools

import jax
import jax.numpy as jnp
from jax import lax
from jax.experimental import pallas as pl
from jax.experimental.pallas import tpu as pltpu
from jax.sharding import PartitionSpec as P

LANGS = 32
MESH = pl.DeviceIdType.MESH
CORES = 2


def layout(dp, mp, ff_local):
    nz = dp // 2 if dp % 2 == 0 else 1
    if ff_local % (128 * nz):
        nz = 1
    return nz, dp // nz, mp // CORES


def gather_kernel(
    nz, ny, nx, x_ref, g_ref, w_ref, v_ref, xa, ga, wa, va, send, tok_recv, wgt_recv, local
):
    d, m = lax.axis_index("dp"), lax.axis_index("mp")
    z, y = d // ny, d % ny
    x, c = m // CORES, m % CORES
    mp = nx * CORES
    rows, feats = x_ref.shape
    depth, ff = w_ref.shape
    part = ff // nz

    def at(zz, yy, xx, cc):
        return (zz * ny + yy, xx * CORES + cc)

    core = at(z, y, x, 1 - c)
    peers = [at(lax.rem(z + k, nz), y, x, c) for k in range(1, nz)]
    peers += [at(z, lax.rem(y + k, ny), x, c) for k in range(1, ny)]
    peers += [at(z, y, lax.rem(x + k, nx), c) for k in range(1, nx)]
    peers += [core]
    barrier = pltpu.get_barrier_semaphore()
    for peer in peers:
        pl.semaphore_signal(barrier, inc=1, device_id=peer, device_id_type=MESH)
    pl.semaphore_wait(barrier, len(peers))

    own_tok, all_tok = (x_ref, g_ref), (xa, ga)
    pending = []

    def tok_slot(a, zz, mm):
        return all_tok[a].at[
            pl.ds(zz * rows if isinstance(zz, int) else pl.multiple_of(zz * rows, rows), rows),
            pl.ds(pl.multiple_of(mm * feats, feats), feats),
        ]

    def tok_sem(a, zz, mm):
        return tok_recv.at[(a * nz + zz) * mp + mm]

    def wgt_cut(w, zz):
        span = pl.ds(zz * part if isinstance(zz, int) else pl.multiple_of(zz * part, part), part)
        return w_ref.at[:, span] if w == 0 else v_ref.at[span, :]

    def wgt_slot(w, dd):
        span = pl.ds(pl.multiple_of(dd * depth, depth), depth)
        return wa.at[span, :] if w == 0 else va.at[:, span]

    def wgt_sem(w, dd):
        return wgt_recv.at[w * nz * ny + dd]

    def push(conds, src, dst, sem, dev, like):
        copy = pltpu.make_async_remote_copy(
            src_ref=src, dst_ref=dst, send_sem=send.at[len(pending)], recv_sem=sem,
            device_id=dev, device_id_type=MESH,
        )
        copy.start()
        pending.append((conds, like))

    def arrived(slot, sem, dev):
        pltpu.make_async_remote_copy(
            src_ref=slot, dst_ref=slot, send_sem=send.at[0], recv_sem=sem,
            device_id=dev, device_id_type=MESH,
        ).wait_recv()

    has_right, has_left = z < nz - 1, z > 0

    def along_z(conds, a, zz, src, right, left):
        for go, step, edge in ((right, 1, has_right), (left, -1, has_left)):
            if go and nz > 1:

                @pl.when(edge)
                def _():
                    slot, sem = tok_slot(a, zz, m), tok_sem(a, zz, m)
                    push(conds + (edge,), src, slot, sem, at(z + step, y, x, c), x_ref)

    def along_x_core(conds, a, zz, src):
        slot, sem = tok_slot(a, zz, m), tok_sem(a, zz, m)
        for k in range(1, nx):
            push(conds, src, slot, sem, at(z, y, lax.rem(x + k, nx), c), x_ref)
        push(conds, src, slot, sem, core, x_ref)

    def x_to_core(conds, a, zz):
        for k in range(1, nx):
            xx = lax.rem(x + k, nx)
            mm = xx * CORES + c
            arrived(tok_slot(a, zz, mm), tok_sem(a, zz, mm), at(z, y, xx, c))
            push(conds, tok_slot(a, zz, mm), tok_slot(a, zz, mm), tok_sem(a, zz, mm), core, x_ref)

    def along_y(w, zz, src):
        dd = zz * ny + y
        for k in range(1, ny):
            dev = at(z, lax.rem(y + k, ny), x, c)
            push((), src, wgt_slot(w, dd), wgt_sem(w, dd), dev, wgt_cut(w, 0))

    def guarded(conds, fn):
        if conds:
            pl.when(functools.reduce(jnp.logical_and, conds))(fn)
        else:
            fn()

    for a in range(2):
        along_z((), a, z, own_tok[a], True, True)
        for k in range(1, nz):
            zz = lax.rem(z + k, nz)
            dev = at(zz, y, x, c)
            push((), wgt_cut(a, zz), wgt_slot(a, d), wgt_sem(a, d), dev, wgt_cut(a, 0))
    mine = []
    for a in range(2):
        along_x_core((), a, z, own_tok[a])
        along_y(a, z, wgt_cut(a, z))
        for j, (src, dst) in enumerate(
            ((own_tok[a], tok_slot(a, z, m)), (wgt_cut(a, z), wgt_slot(a, d)))
        ):
            copy = pltpu.make_async_copy(src, dst, local.at[a * 2 + j])
            copy.start()
            mine.append(copy)

    late = [((), a, z) for a in range(2)]

    def drain():
        while late:
            conds, a, zz = late.pop(0)
            guarded(conds, functools.partial(x_to_core, conds, a, zz))

    for s in range(1, nz):
        for a in range(2):
            fresh = []
            for cond, zz, near, right in (
                (z >= s, z - s, z - 1, True), (z + s < nz, z + s, z + 1, False)
            ):
                def relay(cond=cond, zz=zz, near=near, right=right):
                    arrived(tok_slot(a, zz, m), tok_sem(a, zz, m), at(near, y, x, c))
                    if s < nz - 1:
                        along_z((cond,), a, zz, tok_slot(a, zz, m), right, not right)
                    along_x_core((cond,), a, zz, tok_slot(a, zz, m))

                pl.when(cond)(relay)
                fresh.append(((cond,), a, zz))
            zz = lax.rem(z - s + nz, nz)
            dd = zz * ny + y
            arrived(wgt_slot(a, dd), wgt_sem(a, dd), at(zz, y, x, c))
            along_y(a, zz, wgt_slot(a, dd))
            drain()
            late.extend(fresh)
    drain()

    for a in range(2):
        for zz in range(nz):
            for k in range(nx):
                mm = k * CORES + 1 - c
                arrived(tok_slot(a, zz, mm), tok_sem(a, zz, mm), core)
            for k in range(1, ny):
                yy = lax.rem(y + k, ny)
                dd = zz * ny + yy
                arrived(wgt_slot(a, dd), wgt_sem(a, dd), at(z, yy, x, c))
    for copy in mine:
        copy.wait()
    for i, (conds, like) in enumerate(pending):
        sent = pltpu.make_async_remote_copy(
            src_ref=like, dst_ref=like, send_sem=send.at[i], recv_sem=tok_recv.at[0],
            device_id=core, device_id_type=MESH,
        )
        guarded(conds, sent.wait_send)


def gather_all(nz, ny, nx, tokens, grads, gate_weight, down_weight):
    rows, feats = tokens.shape
    depth, ff = gate_weight.shape
    mp, dp = nx * CORES, nz * ny
    part = ff // nz
    sends = 2 * (2 * nz + nz * (nx - 1) + nz * nx + nz + nz * ny + 2 * nz * nx) * 2
    shapes = [(nz * rows, mp * feats)] * 2 + [(dp * depth, part), (part, dp * depth)]
    anywhere = pl.BlockSpec(memory_space=pl.ANY)
    return pl.pallas_call(
        functools.partial(gather_kernel, nz, ny, nx),
        out_shape=[jax.ShapeDtypeStruct(s, jnp.bfloat16) for s in shapes],
        in_specs=[anywhere] * 4,
        out_specs=[anywhere] * 4,
        scratch_shapes=[
            pltpu.SemaphoreType.DMA((sends,)),
            pltpu.SemaphoreType.DMA((2 * nz * mp,)),
            pltpu.SemaphoreType.DMA((2 * dp,)),
            pltpu.SemaphoreType.DMA((4,)),
        ],
        compiler_params=pltpu.CompilerParams(collective_id=0, has_side_effects=True),
        name="gather_all",
    )(tokens, grads, gate_weight, down_weight)


def shards(
    inputs, out_grads, gate_weight, down_weight, in_proj, out_proj, in_precond, out_precond,
    queries, languages,
):
    dp, mp = lax.axis_size("dp"), lax.axis_size("mp")
    nz, ny, nx = layout(dp, mp, gate_weight.shape[1])
    local_ex, seq_len, feats = inputs.shape
    rank = in_proj.shape[1]
    per_language = languages.shape[0] * dp // LANGS
    exact = lax.Precision.HIGHEST

    onehot = (languages[None, :] == jnp.arange(LANGS, dtype=jnp.int32)[:, None])
    lang_sum = jnp.dot(
        onehot.astype(jnp.bfloat16), queries, preferred_element_type=jnp.float32
    )
    lang_sum = lax.psum(lang_sum, "dp")
    lang_sum = lax.all_gather(lang_sum, "mp", axis=1, tiled=True)
    lang_sum = lang_sum.reshape(LANGS, rank, rank)
    turned = jnp.einsum("lij,bj->lib", lang_sum, out_precond, precision=exact)
    turned = jnp.einsum("ia,lib->lab", in_precond, turned, precision=exact)
    turned = turned / (seq_len * per_language)

    tok, grd, gate_all, down_all = gather_all(
        nz, ny, nx,
        inputs.reshape(local_ex * seq_len, feats),
        out_grads.reshape(local_ex * seq_len, feats),
        gate_weight, down_weight,
    )
    gate = jnp.dot(tok, gate_all, preferred_element_type=jnp.float32)
    hidden_grad = lax.dot_general(
        grd, down_all, (((1,), (1,)), ((), ())), preferred_element_type=jnp.float32
    )
    up_grad = (hidden_grad * jax.nn.silu(gate)).astype(jnp.bfloat16)
    part = gate_all.shape[1]
    d = lax.axis_index("dp")
    z, y = d // ny, d % ny
    proj = lax.dynamic_slice_in_dim(out_proj, z * part, part, 0)
    out_part = jnp.dot(up_grad, proj, preferred_element_type=jnp.float32)
    in_part = jnp.dot(tok, in_proj, preferred_element_type=jnp.float32)
    cross = jnp.einsum(
        "esa,esb->eab",
        in_part.reshape(nz * local_ex, seq_len, rank),
        out_part.reshape(nz * local_ex, seq_len, rank),
        precision=exact,
    )
    partial = jnp.einsum("eab,lab->el", cross, turned, precision=exact)
    spread = jnp.arange(ny)[None, :, None, None] == y
    spread = jnp.where(spread, partial.reshape(nz, 1, local_ex, LANGS), 0.0)
    total = lax.psum(spread.reshape(dp * local_ex, LANGS), ("dp", "mp"))
    return lax.dynamic_slice_in_dim(total, d * local_ex, local_ex, 0)


def solution(mesh):
    return jax.shard_map(
        shards,
        mesh=mesh,
        in_specs=(
            P("dp", None, "mp"),
            P("dp", None, "mp"),
            P("dp", "mp"),
            P("mp", "dp"),
            P(),
            P("mp", None),
            P(),
            P(),
            P("dp", "mp"),
            P("dp"),
        ),
        out_specs=P("dp", None),
        check_vma=False,
    )
```

```python
import functools

import jax
import jax.numpy as jnp
from jax import lax
from jax.experimental import pallas as pl
from jax.experimental.pallas import tpu as pltpu
from jax.sharding import PartitionSpec as P

LANGS = 32
MESH = pl.DeviceIdType.MESH
CORES = 2


def layout(dp, mp, ff_local):
    nz = dp // 2 if dp % 2 == 0 else 1
    if ff_local % (128 * nz):
        nz = 1
    return nz, dp // nz, mp // CORES


def gather_kernel(
    nz, ny, nx, x_ref, g_ref, w_ref, v_ref, ip_ref, op_ref, a_out, b_out, xa, ga,
    wa, va, silu, buf, send, tok_recv, wgt_recv, local, load_sem,
):
    d, m = lax.axis_index("dp"), lax.axis_index("mp")
    z, y = d // ny, d % ny
    x, c = m // CORES, m % CORES
    mp = nx * CORES
    rows, feats = x_ref.shape
    depth, ff = w_ref.shape
    part = ff // nz

    def at(zz, yy, xx, cc):
        return (zz * ny + yy, xx * CORES + cc)

    core = at(z, y, x, 1 - c)
    peers = [at(lax.rem(z + k, nz), y, x, c) for k in range(1, nz)]
    peers += [at(z, lax.rem(y + k, ny), x, c) for k in range(1, ny)]
    peers += [at(z, y, lax.rem(x + k, nx), c) for k in range(1, nx)]
    peers += [core]
    barrier = pltpu.get_barrier_semaphore()
    for peer in peers:
        pl.semaphore_signal(barrier, inc=1, device_id=peer, device_id_type=MESH)
    pl.semaphore_wait(barrier, len(peers))

    own_tok, all_tok = (x_ref, g_ref), (xa, ga)
    pending = []

    def tok_slot(a, zz, mm):
        return all_tok[a].at[
            pl.ds(zz * rows if isinstance(zz, int) else pl.multiple_of(zz * rows, rows), rows),
            pl.ds(pl.multiple_of(mm * feats, feats), feats),
        ]

    def tok_sem(a, zz, mm):
        return tok_recv.at[(a * nz + zz) * mp + mm]

    def wgt_cut(w, zz):
        span = pl.ds(zz * part if isinstance(zz, int) else pl.multiple_of(zz * part, part), part)
        return w_ref.at[:, span] if w == 0 else v_ref.at[span, :]

    def wgt_slot(w, dd):
        span = pl.ds(pl.multiple_of(dd * depth, depth), depth)
        return wa.at[span, :] if w == 0 else va.at[:, span]

    def wgt_sem(w, dd):
        return wgt_recv.at[w * nz * ny + dd]

    def push(conds, src, dst, sem, dev, like):
        copy = pltpu.make_async_remote_copy(
            src_ref=src, dst_ref=dst, send_sem=send.at[len(pending)], recv_sem=sem,
            device_id=dev, device_id_type=MESH,
        )
        copy.start()
        pending.append((conds, like))

    def arrived(slot, sem, dev):
        pltpu.make_async_remote_copy(
            src_ref=slot, dst_ref=slot, send_sem=send.at[0], recv_sem=sem,
            device_id=dev, device_id_type=MESH,
        ).wait_recv()

    has_right, has_left = z < nz - 1, z > 0

    def along_z(conds, a, zz, src, right, left):
        for go, step, edge in ((right, 1, has_right), (left, -1, has_left)):
            if go and nz > 1:

                @pl.when(edge)
                def _():
                    slot, sem = tok_slot(a, zz, m), tok_sem(a, zz, m)
                    push(conds + (edge,), src, slot, sem, at(z + step, y, x, c), x_ref)

    def along_x_core(conds, a, zz, src):
        slot, sem = tok_slot(a, zz, m), tok_sem(a, zz, m)
        for k in range(1, nx):
            push(conds, src, slot, sem, at(z, y, lax.rem(x + k, nx), c), x_ref)
        push(conds, src, slot, sem, core, x_ref)

    def x_to_core(conds, a, zz):
        for k in range(1, nx):
            xx = lax.rem(x + k, nx)
            mm = xx * CORES + c
            arrived(tok_slot(a, zz, mm), tok_sem(a, zz, mm), at(z, y, xx, c))
            push(conds, tok_slot(a, zz, mm), tok_slot(a, zz, mm), tok_sem(a, zz, mm), core, x_ref)

    def along_y(w, zz, src):
        dd = zz * ny + y
        for k in range(1, ny):
            dev = at(z, lax.rem(y + k, ny), x, c)
            push((), src, wgt_slot(w, dd), wgt_sem(w, dd), dev, wgt_cut(w, 0))

    def guarded(conds, fn):
        if conds:
            pl.when(functools.reduce(jnp.logical_and, conds))(fn)
        else:
            fn()

    def own_along_z(a):
        along_z((), a, z, own_tok[a], True, True)

    def own_cuts(a):
        for k in range(1, nz):
            zz = lax.rem(z + k, nz)
            dev = at(zz, y, x, c)
            push((), wgt_cut(a, zz), wgt_slot(a, d), wgt_sem(a, d), dev, wgt_cut(a, 0))

    mine = []

    def own_rest(a):
        along_x_core((), a, z, own_tok[a])
        along_y(a, z, wgt_cut(a, z))
        for j, (src, dst) in enumerate(
            ((own_tok[a], tok_slot(a, z, m)), (wgt_cut(a, z), wgt_slot(a, d)))
        ):
            copy = pltpu.make_async_copy(src, dst, local.at[a * 2 + j])
            copy.start()
            mine.append(copy)

    late = []

    def drain():
        while late:
            conds, a, zz = late.pop(0)
            guarded(conds, functools.partial(x_to_core, conds, a, zz))

    def relay_tokens(a, s):
        fresh = []
        for cond, zz, near, right in (
            (z >= s, z - s, z - 1, True), (z + s < nz, z + s, z + 1, False)
        ):
            def relay(cond=cond, zz=zz, near=near, right=right):
                arrived(tok_slot(a, zz, m), tok_sem(a, zz, m), at(near, y, x, c))
                if s < nz - 1:
                    along_z((cond,), a, zz, tok_slot(a, zz, m), right, not right)
                along_x_core((cond,), a, zz, tok_slot(a, zz, m))

            pl.when(cond)(relay)
            fresh.append(((cond,), a, zz))
        drain()
        late.extend(fresh)

    def relay_cuts(w, s):
        zz = lax.rem(z - s + nz, nz)
        dd = zz * ny + y
        arrived(wgt_slot(w, dd), wgt_sem(w, dd), at(zz, y, x, c))
        along_y(w, zz, wgt_slot(w, dd))

    def rest_of_cuts(w):
        for zz in range(nz):
            for k in range(1, ny):
                yy = lax.rem(y + k, ny)
                dd = zz * ny + yy
                arrived(wgt_slot(w, dd), wgt_sem(w, dd), at(z, yy, x, c))
        mine[2 * w + 1].wait()

    def rest_of_tokens(a):
        for zz in range(nz):
            for k in range(nx):
                mm = k * CORES + 1 - c
                arrived(tok_slot(a, zz, mm), tok_sem(a, zz, mm), core)
        mine[2 * a].wait()

    def load(a, e):
        span = pl.ds(pl.multiple_of(e * rows, rows), rows)
        return pltpu.make_async_copy(all_tok[a].at[span, :], buf.at[lax.rem(e, 2)], load_sem.at[lax.rem(e, 2)])

    tile = 256
    whole_tiles, rest = part // tile, part % tile

    def over_examples(a, step):
        load(a, 0).start()

        @pl.loop(0, nz)
        def _(e):
            load(a, e).wait()

            @pl.when(e + 1 < nz)
            def _():
                load(a, e + 1).start()

            block = buf.at[lax.rem(e, 2)]
            out_rows = pl.ds(pl.multiple_of(e * rows, rows), rows)
            step(block, out_rows)

    def over_tiles(step):
        if whole_tiles:

            @pl.loop(0, whole_tiles)
            def _(j):
                step(pl.ds(pl.multiple_of(j * tile, tile), tile))

        if rest:
            step(pl.ds(whole_tiles * tile, rest))

    def gate_step(block, out_rows):
        a_out[out_rows, :] = jnp.dot(block[...], ip_ref[...], preferred_element_type=jnp.float32)

        def cols(span):
            v = jnp.dot(block[...], wa[:, span], preferred_element_type=jnp.float32)
            silu[out_rows, span] = v / (1.0 + jnp.exp(-v))

        over_tiles(cols)

    def hidden_step(block, out_rows):
        b_out[out_rows, :] = jnp.zeros((rows, b_out.shape[1]), jnp.float32)

        def cols(span):
            grad = lax.dot_general(
                block[...], va[span, :], (((1,), (1,)), ((), ())),
                preferred_element_type=jnp.float32,
            )
            up = (grad * silu[out_rows, span]).astype(jnp.bfloat16)
            b_out[out_rows, :] += jnp.dot(up, op_ref[span, :], preferred_element_type=jnp.float32)

        over_tiles(cols)

    own_along_z(0)
    own_cuts(0)
    own_rest(0)
    own_along_z(1)
    own_cuts(1)
    own_rest(1)
    late.append(((), 0, z))
    for s in range(1, nz):
        relay_tokens(0, s)
        relay_cuts(0, s)
        if s == 1:
            relay_tokens(1, 1)
    drain()
    if nz > 2:
        relay_tokens(1, 2)
    rest_of_cuts(0)
    rest_of_tokens(0)
    over_examples(0, gate_step)
    late.append(((), 1, z))
    for s in range(1, nz):
        relay_cuts(1, s)
        if s > 2:
            relay_tokens(1, s)
    drain()
    rest_of_cuts(1)
    rest_of_tokens(1)
    over_examples(1, hidden_step)

    for i, (conds, like) in enumerate(pending):
        sent = pltpu.make_async_remote_copy(
            src_ref=like, dst_ref=like, send_sem=send.at[i], recv_sem=tok_recv.at[0],
            device_id=core, device_id_type=MESH,
        )
        guarded(conds, sent.wait_send)


def factors(nz, ny, nx, tokens, grads, gate_weight, down_weight, in_proj, out_proj):
    rows, feats = tokens.shape
    depth, ff = gate_weight.shape
    mp, dp = nx * CORES, nz * ny
    part = ff // nz
    rank = in_proj.shape[1]
    sends = 2 * (4 * nz + 2 * nz * (nx - 1) + 4 * nz * nx + nz + nz * ny)
    anywhere = pl.BlockSpec(memory_space=pl.ANY)
    vmem = pl.BlockSpec(memory_space=pltpu.VMEM)
    factor = jax.ShapeDtypeStruct((nz * rows, rank), jnp.float32)
    gathered = jax.ShapeDtypeStruct((nz * rows, mp * feats), jnp.bfloat16)
    in_part, out_part, _, _ = pl.pallas_call(
        functools.partial(gather_kernel, nz, ny, nx),
        out_shape=[factor, factor, gathered, gathered],
        in_specs=[anywhere] * 4 + [vmem] * 2,
        out_specs=[vmem] * 2 + [anywhere] * 2,
        scratch_shapes=[
            pltpu.VMEM((dp * depth, part), jnp.bfloat16),
            pltpu.VMEM((part, dp * depth), jnp.bfloat16),
            pltpu.VMEM((nz * rows, part), jnp.float32),
            pltpu.VMEM((2, rows, mp * feats), jnp.bfloat16),
            pltpu.SemaphoreType.DMA((sends,)),
            pltpu.SemaphoreType.DMA((2 * nz * mp,)),
            pltpu.SemaphoreType.DMA((2 * dp,)),
            pltpu.SemaphoreType.DMA((4,)),
            pltpu.SemaphoreType.DMA((2,)),
        ],
        compiler_params=pltpu.CompilerParams(
            collective_id=0, has_side_effects=True, vmem_limit_bytes=52 * 2**20
        ),
        name="factors",
    )(tokens, grads, gate_weight, down_weight, in_proj, out_proj)
    return in_part, out_part


def sum_kernel(nz, ny, nx, part_ref, out_ref, slots, send, recv):
    d, m = lax.axis_index("dp"), lax.axis_index("mp")
    z, y = d // ny, d % ny
    mp = nx * CORES
    count = nz * mp
    me = z * mp + m

    def device(i):
        return (i // mp * ny + y, lax.rem(i, mp))

    barrier = pltpu.get_barrier_semaphore()
    for k in range(1, count):
        peer = device(lax.rem(me + k, count))
        pl.semaphore_signal(barrier, inc=1, device_id=peer, device_id_type=MESH)
    slots[me] = part_ref[...]
    pl.semaphore_wait(barrier, count - 1)

    def copy(k, to, into):
        return pltpu.make_async_remote_copy(
            src_ref=part_ref, dst_ref=slots.at[into], send_sem=send.at[k],
            recv_sem=recv.at[into], device_id=device(to), device_id_type=MESH,
        )

    for k in range(1, count):
        copy(k, lax.rem(me + k, count), me).start()
    for k in range(1, count):
        other = lax.rem(me + count - k, count)
        copy(k, other, other).wait_recv()
    total = slots[0]
    for i in range(1, count):
        total = total + slots[i]
    out_ref[...] = total
    for k in range(1, count):
        copy(k, lax.rem(me + k, count), me).wait_send()


def sum_over_parts(nz, ny, nx, tile):
    count = nz * nx * CORES
    vmem = pl.BlockSpec(memory_space=pltpu.VMEM)
    return pl.pallas_call(
        functools.partial(sum_kernel, nz, ny, nx),
        out_shape=jax.ShapeDtypeStruct(tile.shape, jnp.float32),
        in_specs=[vmem],
        out_specs=vmem,
        scratch_shapes=[
            pltpu.VMEM((count,) + tile.shape, jnp.float32),
            pltpu.SemaphoreType.DMA((count,)),
            pltpu.SemaphoreType.DMA((count,)),
        ],
        compiler_params=pltpu.CompilerParams(collective_id=1, has_side_effects=True),
        name="sum_over_parts",
    )(tile)


def shards(
    inputs, out_grads, gate_weight, down_weight, in_proj, out_proj, in_precond, out_precond,
    queries, languages,
):
    dp, mp = lax.axis_size("dp"), lax.axis_size("mp")
    nz, ny, nx = layout(dp, mp, gate_weight.shape[1])
    local_ex, seq_len, feats = inputs.shape
    rank = in_proj.shape[1]
    per_language = languages.shape[0] * dp // LANGS
    exact = lax.Precision.HIGHEST

    onehot = (languages[None, :] == jnp.arange(LANGS, dtype=jnp.int32)[:, None])
    lang_sum = jnp.dot(
        onehot.astype(jnp.bfloat16), queries, preferred_element_type=jnp.float32
    )
    lang_sum = lax.psum(lang_sum, "dp")
    lang_sum = lax.all_gather(lang_sum, "mp", axis=1, tiled=True)
    lang_sum = lang_sum.reshape(LANGS, rank, rank)
    turned = jnp.einsum("lij,bj->lib", lang_sum, out_precond, precision=exact)
    turned = jnp.einsum("ia,lib->lab", in_precond, turned, precision=exact)
    turned = turned / (seq_len * per_language)

    part = gate_weight.shape[1] // nz
    z = lax.axis_index("dp") // ny
    in_part, out_part = factors(
        nz, ny, nx,
        inputs.reshape(local_ex * seq_len, feats),
        out_grads.reshape(local_ex * seq_len, feats),
        gate_weight, down_weight, in_proj,
        lax.dynamic_slice_in_dim(out_proj, z * part, part, 0),
    )
    cross = jnp.einsum(
        "esa,esb->eab",
        in_part.reshape(nz * local_ex, seq_len, rank),
        out_part.reshape(nz * local_ex, seq_len, rank),
        precision=exact,
    )
    partial = jnp.einsum("eab,lab->el", cross, turned, precision=exact)
    held = nz * local_ex
    tile = jnp.pad(partial, ((0, -held % 8), (0, -LANGS % 128)))
    total = sum_over_parts(nz, ny, nx, tile)[:, :LANGS]
    return lax.dynamic_slice_in_dim(total, z * local_ex, local_ex, 0)


def solution(mesh):
    return jax.shard_map(
        shards,
        mesh=mesh,
        in_specs=(
            P("dp", None, "mp"),
            P("dp", None, "mp"),
            P("dp", "mp"),
            P("mp", "dp"),
            P(),
            P("mp", None),
            P(),
            P(),
            P("dp", "mp"),
            P("dp"),
        ),
        out_specs=P("dp", None),
        check_vma=False,
    )
```

```python
import functools

import jax
import jax.numpy as jnp
from jax import lax
from jax.experimental import pallas as pl
from jax.experimental.pallas import tpu as pltpu
from jax.sharding import PartitionSpec as P

LANGS = 32
MESH = pl.DeviceIdType.MESH
CORES = 2
TILE = 256


def layout(dp, mp, ff_local):
    nz = dp // 2 if dp % 2 == 0 else 1
    if ff_local % (128 * nz):
        nz = 1
    return nz, dp // nz, mp // CORES


def cuts_of(part):
    first = min(part, (part // 2 + TILE - 1) // TILE * TILE)
    spans = [(0, part), (0, first)]
    return spans + [(first, part - first)] if first < part else spans


def gather_kernel(
    nz, ny, nx, x_ref, g_ref, w_ref, v_ref, ip_ref, op_ref, a_out, b_out, xa, ga,
    wa, va, silu, buf, send, tok_recv, wgt_recv, local, load_sem,
):
    d, m = lax.axis_index("dp"), lax.axis_index("mp")
    z, y = d // ny, d % ny
    x, c = m // CORES, m % CORES
    mp = nx * CORES
    rows, feats = x_ref.shape
    depth, ff = w_ref.shape
    part = ff // nz
    cut_spans = cuts_of(part)

    def at(zz, yy, xx, cc):
        return (zz * ny + yy, xx * CORES + cc)

    core = at(z, y, x, 1 - c)
    peers = [at(lax.rem(z + k, nz), y, x, c) for k in range(1, nz)]
    peers += [at(z, lax.rem(y + k, ny), x, c) for k in range(1, ny)]
    peers += [at(z, y, lax.rem(x + k, nx), c) for k in range(1, nx)]
    peers += [core]
    barrier = pltpu.get_barrier_semaphore()
    for peer in peers:
        pl.semaphore_signal(barrier, inc=1, device_id=peer, device_id_type=MESH)
    pl.semaphore_wait(barrier, len(peers))

    own_tok, all_tok = (x_ref, g_ref), (xa, ga)
    pending = []

    def tok_slot(a, zz, mm):
        return all_tok[a].at[
            pl.ds(zz * rows if isinstance(zz, int) else pl.multiple_of(zz * rows, rows), rows),
            pl.ds(pl.multiple_of(mm * feats, feats), feats),
        ]

    def tok_sem(a, zz, mm):
        return tok_recv.at[(a * nz + zz) * mp + mm]

    def wgt_cut(w, zz):
        lo, size = cut_spans[w]
        span = pl.ds(zz * part + lo if isinstance(zz, int) else pl.multiple_of(zz * part + lo, 128), size)
        return w_ref.at[:, span] if w == 0 else v_ref.at[span, :]

    def wgt_slot(w, dd):
        lo, size = cut_spans[w]
        span = pl.ds(pl.multiple_of(dd * depth, depth), depth)
        return wa.at[span, pl.ds(0, part)] if w == 0 else va.at[pl.ds(lo, size), span]

    def wgt_sem(w, dd):
        return wgt_recv.at[w * nz * ny + dd]

    def push(conds, src, dst, sem, dev, like):
        copy = pltpu.make_async_remote_copy(
            src_ref=src, dst_ref=dst, send_sem=send.at[len(pending)], recv_sem=sem,
            device_id=dev, device_id_type=MESH,
        )
        copy.start()
        pending.append((conds, like))

    def arrived(slot, sem, dev):
        pltpu.make_async_remote_copy(
            src_ref=slot, dst_ref=slot, send_sem=send.at[0], recv_sem=sem,
            device_id=dev, device_id_type=MESH,
        ).wait_recv()

    has_right, has_left = z < nz - 1, z > 0

    def along_z(conds, a, zz, src, right, left):
        for go, step, edge in ((right, 1, has_right), (left, -1, has_left)):
            if go and nz > 1:

                @pl.when(edge)
                def _():
                    slot, sem = tok_slot(a, zz, m), tok_sem(a, zz, m)
                    push(conds + (edge,), src, slot, sem, at(z + step, y, x, c), x_ref)

    def along_x_core(conds, a, zz, src):
        slot, sem = tok_slot(a, zz, m), tok_sem(a, zz, m)
        for k in range(1, nx):
            push(conds, src, slot, sem, at(z, y, lax.rem(x + k, nx), c), x_ref)
        push(conds, src, slot, sem, core, x_ref)

    def x_to_core(conds, a, zz):
        for k in range(1, nx):
            xx = lax.rem(x + k, nx)
            mm = xx * CORES + c
            arrived(tok_slot(a, zz, mm), tok_sem(a, zz, mm), at(z, y, xx, c))
            push(conds, tok_slot(a, zz, mm), tok_slot(a, zz, mm), tok_sem(a, zz, mm), core, x_ref)

    def along_y(w, zz, src):
        dd = zz * ny + y
        for k in range(1, ny):
            dev = at(z, lax.rem(y + k, ny), x, c)
            push((), src, wgt_slot(w, dd), wgt_sem(w, dd), dev, wgt_cut(w, 0))

    def guarded(conds, fn):
        if conds:
            pl.when(functools.reduce(jnp.logical_and, conds))(fn)
        else:
            fn()

    def own_along_z(a):
        along_z((), a, z, own_tok[a], True, True)

    def own_cuts(a):
        for k in range(1, nz):
            zz = lax.rem(z + k, nz)
            dev = at(zz, y, x, c)
            push((), wgt_cut(a, zz), wgt_slot(a, d), wgt_sem(a, d), dev, wgt_cut(a, 0))

    own_copies = {}

    def keep(key, src, dst):
        own_copies[key] = pltpu.make_async_copy(src, dst, local.at[len(own_copies)])
        own_copies[key].start()

    def own_tokens(a):
        along_x_core((), a, z, own_tok[a])
        keep(("tokens", a), own_tok[a], tok_slot(a, z, m))
        late.append(((), a, z))

    def own_weights(w):
        along_y(w, z, wgt_cut(w, z))
        keep(("cut", w), wgt_cut(w, z), wgt_slot(w, d))

    late = []

    def drain():
        while late:
            conds, a, zz = late.pop(0)
            guarded(conds, functools.partial(x_to_core, conds, a, zz))

    def relay_tokens(a, s):
        fresh = []
        for cond, zz, near, right in (
            (z >= s, z - s, z - 1, True), (z + s < nz, z + s, z + 1, False)
        ):
            def relay(cond=cond, zz=zz, near=near, right=right):
                arrived(tok_slot(a, zz, m), tok_sem(a, zz, m), at(near, y, x, c))
                if s < nz - 1:
                    along_z((cond,), a, zz, tok_slot(a, zz, m), right, not right)
                along_x_core((cond,), a, zz, tok_slot(a, zz, m))

            pl.when(cond)(relay)
            fresh.append(((cond,), a, zz))
        drain()
        late.extend(fresh)

    def relay_cuts(w, s):
        zz = lax.rem(z - s + nz, nz)
        dd = zz * ny + y
        arrived(wgt_slot(w, dd), wgt_sem(w, dd), at(zz, y, x, c))
        along_y(w, zz, wgt_slot(w, dd))

    def rest_of_cuts(w):
        for zz in range(nz):
            for k in range(1, ny):
                yy = lax.rem(y + k, ny)
                dd = zz * ny + yy
                arrived(wgt_slot(w, dd), wgt_sem(w, dd), at(z, yy, x, c))
        own_copies["cut", w].wait()

    def rest_of_tokens(a):
        for zz in range(nz):
            for k in range(nx):
                mm = k * CORES + 1 - c
                arrived(tok_slot(a, zz, mm), tok_sem(a, zz, mm), core)
        own_copies["tokens", a].wait()

    def load(a, e):
        return pltpu.make_async_copy(
            all_tok[a].at[pl.ds(e * rows, rows), :], buf.at[e % 2], load_sem.at[e % 2]
        )

    def example(a, e):
        if e == 0:
            load(a, 0).start()
        load(a, e).wait()
        if e + 1 < nz:
            load(a, e + 1).start()
        return buf.at[e % 2], pl.ds(e * rows, rows)

    def over_tiles(lo, size, step):
        whole = size // TILE
        if whole:

            @pl.loop(0, whole)
            def _(j):
                step(pl.ds(pl.multiple_of(lo + j * TILE, TILE), TILE))

        if size % TILE:
            step(pl.ds(lo + whole * TILE, size % TILE))

    def gate_step(e):
        block, out_rows = example(0, e)
        last = part // TILE * TILE
        wide = part - last

        def cols(span):
            v = jnp.dot(block[...], wa[:, span], preferred_element_type=jnp.float32)
            silu[out_rows, span] = v / (1.0 + jnp.exp(-v))

        over_tiles(0, last, cols)
        v = jnp.dot(block[...], wa[:, last:], preferred_element_type=jnp.float32)
        if wide:
            gate = v[:, :wide]
            silu[out_rows, last:part] = gate / (1.0 + jnp.exp(-gate))
        a_out[out_rows, :] = v[:, wide:]

    def hidden_step(w, e):
        block, out_rows = example(1, e)
        if w == 1:
            b_out[out_rows, :] = jnp.zeros((rows, b_out.shape[1]), jnp.float32)

        def cols(span):
            grad = lax.dot_general(
                block[...], va[span, :], (((1,), (1,)), ((), ())),
                preferred_element_type=jnp.float32,
            )
            up = (grad * silu[out_rows, span]).astype(jnp.bfloat16)
            b_out[out_rows, :] += jnp.dot(up, op_ref[span, :], preferred_element_type=jnp.float32)

        over_tiles(*cut_spans[w], cols)

    own_along_z(0)
    own_along_z(1)
    own_tokens(0)
    own_tokens(1)
    own_cuts(0)
    own_weights(0)
    wa[:, part:] = ip_ref[...]
    down = range(1, len(cut_spans))
    for s in range(1, nz):
        relay_tokens(0, s)
        relay_tokens(1, s)
        if s == 1:
            for w in down:
                own_cuts(w)
        if s > 1:
            relay_cuts(0, s - 1)
    for w in down:
        own_weights(w)
    if nz > 1:
        relay_cuts(0, nz - 1)
    drain()
    rest_of_cuts(0)
    rest_of_tokens(0)
    steps = [(w, s) for w in down for s in range(1, nz)]
    for e in range(nz):
        gate_step(e)
        if e < nz - 1:
            relay_cuts(*steps.pop(0))
    for w, s in steps:
        relay_cuts(w, s)
    rest_of_tokens(1)
    for w in down:
        rest_of_cuts(w)
        for e in range(nz):
            hidden_step(w, e)

    for i, (conds, like) in enumerate(pending):
        sent = pltpu.make_async_remote_copy(
            src_ref=like, dst_ref=like, send_sem=send.at[i], recv_sem=tok_recv.at[0],
            device_id=core, device_id_type=MESH,
        )
        guarded(conds, sent.wait_send)


def factors(nz, ny, nx, tokens, grads, gate_weight, down_weight, in_proj, out_proj):
    rows, feats = tokens.shape
    depth, ff = gate_weight.shape
    mp, dp = nx * CORES, nz * ny
    part = ff // nz
    rank = in_proj.shape[1]
    sends = 2 * (4 * nz + 2 * nz * (nx - 1) + 4 * nz * nx) + 3 * (nz + nz * ny)
    in_wide = jnp.pad(in_proj, ((0, 0), (0, -rank % 128)))
    wide = in_wide.shape[1]
    anywhere = pl.BlockSpec(memory_space=pl.ANY)
    vmem = pl.BlockSpec(memory_space=pltpu.VMEM)
    in_factor = jax.ShapeDtypeStruct((nz * rows, wide), jnp.float32)
    out_factor = jax.ShapeDtypeStruct((nz * rows, rank), jnp.float32)
    gathered = jax.ShapeDtypeStruct((nz * rows, mp * feats), jnp.bfloat16)
    in_part, out_part, _, _ = pl.pallas_call(
        functools.partial(gather_kernel, nz, ny, nx),
        out_shape=[in_factor, out_factor, gathered, gathered],
        in_specs=[anywhere] * 4 + [vmem] * 2,
        out_specs=[vmem] * 2 + [anywhere] * 2,
        scratch_shapes=[
            pltpu.VMEM((dp * depth, part + wide), jnp.bfloat16),
            pltpu.VMEM((part, dp * depth), jnp.bfloat16),
            pltpu.VMEM((nz * rows, part), jnp.float32),
            pltpu.VMEM((2, rows, mp * feats), jnp.bfloat16),
            pltpu.SemaphoreType.DMA((sends,)),
            pltpu.SemaphoreType.DMA((2 * nz * mp,)),
            pltpu.SemaphoreType.DMA((3 * dp,)),
            pltpu.SemaphoreType.DMA((5,)),
            pltpu.SemaphoreType.DMA((2,)),
        ],
        compiler_params=pltpu.CompilerParams(
            collective_id=0, has_side_effects=True, vmem_limit_bytes=52 * 2**20
        ),
        name="factors",
    )(tokens, grads, gate_weight, down_weight, in_wide, out_proj)
    return in_part[:, :rank], out_part


def sum_kernel(nz, ny, nx, part_ref, out_ref, slots, send, recv):
    d, m = lax.axis_index("dp"), lax.axis_index("mp")
    z, y = d // ny, d % ny
    mp = nx * CORES
    count = nz * mp
    me = z * mp + m

    def device(i):
        return (i // mp * ny + y, lax.rem(i, mp))

    barrier = pltpu.get_barrier_semaphore()
    for k in range(1, count):
        peer = device(lax.rem(me + k, count))
        pl.semaphore_signal(barrier, inc=1, device_id=peer, device_id_type=MESH)
    slots[me] = part_ref[...]
    pl.semaphore_wait(barrier, count - 1)

    def copy(k, to, into):
        return pltpu.make_async_remote_copy(
            src_ref=part_ref, dst_ref=slots.at[into], send_sem=send.at[k],
            recv_sem=recv.at[into], device_id=device(to), device_id_type=MESH,
        )

    for k in range(1, count):
        copy(k, lax.rem(me + k, count), me).start()
    for k in range(1, count):
        other = lax.rem(me + count - k, count)
        copy(k, other, other).wait_recv()
    total = slots[0]
    for i in range(1, count):
        total = total + slots[i]
    out_ref[...] = total
    for k in range(1, count):
        copy(k, lax.rem(me + k, count), me).wait_send()


def sum_over_parts(nz, ny, nx, tile):
    count = nz * nx * CORES
    vmem = pl.BlockSpec(memory_space=pltpu.VMEM)
    return pl.pallas_call(
        functools.partial(sum_kernel, nz, ny, nx),
        out_shape=jax.ShapeDtypeStruct(tile.shape, jnp.float32),
        in_specs=[vmem],
        out_specs=vmem,
        scratch_shapes=[
            pltpu.VMEM((count,) + tile.shape, jnp.float32),
            pltpu.SemaphoreType.DMA((count,)),
            pltpu.SemaphoreType.DMA((count,)),
        ],
        compiler_params=pltpu.CompilerParams(collective_id=1, has_side_effects=True),
        name="sum_over_parts",
    )(tile)


def shards(
    inputs, out_grads, gate_weight, down_weight, in_proj, out_proj, in_precond, out_precond,
    queries, languages,
):
    dp, mp = lax.axis_size("dp"), lax.axis_size("mp")
    nz, ny, nx = layout(dp, mp, gate_weight.shape[1])
    local_ex, seq_len, feats = inputs.shape
    rank = in_proj.shape[1]
    per_language = languages.shape[0] * dp // LANGS
    exact = lax.Precision.HIGHEST

    onehot = (languages[None, :] == jnp.arange(LANGS, dtype=jnp.int32)[:, None])
    lang_sum = jnp.dot(
        onehot.astype(jnp.bfloat16), queries, preferred_element_type=jnp.float32
    )
    lang_sum = lax.psum(lang_sum, "dp")
    lang_sum = lax.all_gather(lang_sum, "mp", axis=1, tiled=True)
    lang_sum = lang_sum.reshape(LANGS, rank, rank)
    turned = jnp.einsum("lij,bj->lib", lang_sum, out_precond, precision=exact)
    turned = jnp.einsum("ia,lib->lab", in_precond, turned, precision=exact)
    turned = turned / (seq_len * per_language)

    part = gate_weight.shape[1] // nz
    z = lax.axis_index("dp") // ny
    in_part, out_part = factors(
        nz, ny, nx,
        inputs.reshape(local_ex * seq_len, feats),
        out_grads.reshape(local_ex * seq_len, feats),
        gate_weight, down_weight, in_proj,
        lax.dynamic_slice_in_dim(out_proj, z * part, part, 0),
    )
    cross = jnp.einsum(
        "esa,esb->eab",
        in_part.reshape(nz * local_ex, seq_len, rank),
        out_part.reshape(nz * local_ex, seq_len, rank),
        precision=exact,
    )
    partial = jnp.einsum("eab,lab->el", cross, turned, precision=exact)
    held = nz * local_ex
    tile = jnp.pad(partial, ((0, -held % 8), (0, -LANGS % 128)))
    total = sum_over_parts(nz, ny, nx, tile)[:, :LANGS]
    return lax.dynamic_slice_in_dim(total, z * local_ex, local_ex, 0)


def solution(mesh):
    return jax.shard_map(
        shards,
        mesh=mesh,
        in_specs=(
            P("dp", None, "mp"),
            P("dp", None, "mp"),
            P("dp", "mp"),
            P("mp", "dp"),
            P(),
            P("mp", None),
            P(),
            P(),
            P("dp", "mp"),
            P("dp"),
        ),
        out_specs=P("dp", None),
        check_vma=False,
    )
```

```python
import functools

import jax
import jax.numpy as jnp
from jax import lax
from jax.experimental import pallas as pl
from jax.experimental.pallas import tpu as pltpu
from jax.sharding import PartitionSpec as P

LANGS = 32
MESH = pl.DeviceIdType.MESH
CORES = 2


def layout(dp, mp, ff_local):
    nz = dp // 2 if dp % 2 == 0 else 1
    if ff_local % (128 * nz):
        nz = 1
    return nz, dp // nz, mp // CORES


def gather_kernel(
    nz, ny, nx, x_ref, g_ref, w_ref, v_ref, xa, ga, wa, va, send, tok_recv, wgt_recv, local
):
    d, m = lax.axis_index("dp"), lax.axis_index("mp")
    z, y = d // ny, d % ny
    x, c = m // CORES, m % CORES
    mp = nx * CORES
    rows, feats = x_ref.shape
    depth, ff = w_ref.shape
    part = ff // nz

    def at(zz, yy, xx, cc):
        return (zz * ny + yy, xx * CORES + cc)

    core = at(z, y, x, 1 - c)
    peers = [at(lax.rem(z + k, nz), y, x, c) for k in range(1, nz)]
    peers += [at(z, lax.rem(y + k, ny), x, c) for k in range(1, ny)]
    peers += [at(z, y, lax.rem(x + k, nx), c) for k in range(1, nx)]
    peers += [core]
    barrier = pltpu.get_barrier_semaphore()
    for peer in peers:
        pl.semaphore_signal(barrier, inc=1, device_id=peer, device_id_type=MESH)
    pl.semaphore_wait(barrier, len(peers))

    own_tok, all_tok = (x_ref, g_ref), (xa, ga)
    pending = []

    def tok_slot(a, zz, mm):
        return all_tok[a].at[
            pl.ds(zz * rows if isinstance(zz, int) else pl.multiple_of(zz * rows, rows), rows),
            pl.ds(pl.multiple_of(mm * feats, feats), feats),
        ]

    def tok_sem(a, zz, mm):
        return tok_recv.at[(a * nz + zz) * mp + mm]

    def wgt_cut(w, zz):
        span = pl.ds(zz * part if isinstance(zz, int) else pl.multiple_of(zz * part, part), part)
        return w_ref.at[:, span] if w == 0 else v_ref.at[span, :]

    def wgt_slot(w, dd):
        span = pl.ds(pl.multiple_of(dd * depth, depth), depth)
        return wa.at[span, :] if w == 0 else va.at[:, span]

    def wgt_sem(w, dd):
        return wgt_recv.at[w * nz * ny + dd]

    def push(conds, src, dst, sem, dev, like):
        copy = pltpu.make_async_remote_copy(
            src_ref=src, dst_ref=dst, send_sem=send.at[len(pending)], recv_sem=sem,
            device_id=dev, device_id_type=MESH,
        )
        copy.start()
        pending.append((conds, like))

    def arrived(slot, sem, dev):
        pltpu.make_async_remote_copy(
            src_ref=slot, dst_ref=slot, send_sem=send.at[0], recv_sem=sem,
            device_id=dev, device_id_type=MESH,
        ).wait_recv()

    has_right, has_left = z < nz - 1, z > 0

    def along_z(conds, a, zz, src, right, left):
        for go, step, edge in ((right, 1, has_right), (left, -1, has_left)):
            if go and nz > 1:

                @pl.when(edge)
                def _():
                    slot, sem = tok_slot(a, zz, m), tok_sem(a, zz, m)
                    push(conds + (edge,), src, slot, sem, at(z + step, y, x, c), x_ref)

    def along_x_core(conds, a, zz, src):
        slot, sem = tok_slot(a, zz, m), tok_sem(a, zz, m)
        for k in range(1, nx):
            push(conds, src, slot, sem, at(z, y, lax.rem(x + k, nx), c), x_ref)
        push(conds, src, slot, sem, core, x_ref)

    def x_to_core(conds, a, zz):
        for k in range(1, nx):
            xx = lax.rem(x + k, nx)
            mm = xx * CORES + c
            arrived(tok_slot(a, zz, mm), tok_sem(a, zz, mm), at(z, y, xx, c))
            push(conds, tok_slot(a, zz, mm), tok_slot(a, zz, mm), tok_sem(a, zz, mm), core, x_ref)

    def along_y(w, zz, src):
        dd = zz * ny + y
        for k in range(1, ny):
            dev = at(z, lax.rem(y + k, ny), x, c)
            push((), src, wgt_slot(w, dd), wgt_sem(w, dd), dev, wgt_cut(w, 0))

    def guarded(conds, fn):
        if conds:
            pl.when(functools.reduce(jnp.logical_and, conds))(fn)
        else:
            fn()

    for a in range(2):
        along_z((), a, z, own_tok[a], True, True)
    for w in range(2):
        for k in range(1, nz):
            zz = lax.rem(z + k, nz)
            dev = at(zz, y, x, c)
            push((), wgt_cut(w, zz), wgt_slot(w, d), wgt_sem(w, d), dev, wgt_cut(w, 0))
    mine = []
    for a in range(2):
        along_x_core((), a, z, own_tok[a])
        along_y(a, z, wgt_cut(a, z))
        for j, (src, dst) in enumerate(
            ((own_tok[a], tok_slot(a, z, m)), (wgt_cut(a, z), wgt_slot(a, d)))
        ):
            copy = pltpu.make_async_copy(src, dst, local.at[a * 2 + j])
            copy.start()
            mine.append(copy)

    late = [((), a, z) for a in range(2)]

    def drain(keep):
        while len(late) > keep:
            conds, a, zz = late.pop(0)
            guarded(conds, functools.partial(x_to_core, conds, a, zz))

    def relay_cuts(s):
        zz = lax.rem(z - s + nz, nz)
        dd = zz * ny + y
        for w in range(2):
            arrived(wgt_slot(w, dd), wgt_sem(w, dd), at(zz, y, x, c))
            along_y(w, zz, wgt_slot(w, dd))

    for s in range(1, nz):
        for a in range(2):
            for cond, zz, near, right in (
                (z >= s, z - s, z - 1, True), (z + s < nz, z + s, z + 1, False)
            ):
                def relay(cond=cond, zz=zz, near=near, right=right):
                    arrived(tok_slot(a, zz, m), tok_sem(a, zz, m), at(near, y, x, c))
                    if s < nz - 1:
                        along_z((cond,), a, zz, tok_slot(a, zz, m), right, not right)
                    along_x_core((cond,), a, zz, tok_slot(a, zz, m))

                pl.when(cond)(relay)
                late.append(((cond,), a, zz))
        if s > 1:
            relay_cuts(s - 1)
        drain(4)
    if nz > 1:
        relay_cuts(nz - 1)
    drain(0)

    for a in range(2):
        for zz in range(nz):
            for k in range(nx):
                mm = k * CORES + 1 - c
                arrived(tok_slot(a, zz, mm), tok_sem(a, zz, mm), core)
            for k in range(1, ny):
                yy = lax.rem(y + k, ny)
                dd = zz * ny + yy
                arrived(wgt_slot(a, dd), wgt_sem(a, dd), at(z, yy, x, c))
    for copy in mine:
        copy.wait()
    for i, (conds, like) in enumerate(pending):
        sent = pltpu.make_async_remote_copy(
            src_ref=like, dst_ref=like, send_sem=send.at[i], recv_sem=tok_recv.at[0],
            device_id=core, device_id_type=MESH,
        )
        guarded(conds, sent.wait_send)


def gather_all(nz, ny, nx, tokens, grads, gate_weight, down_weight):
    rows, feats = tokens.shape
    depth, ff = gate_weight.shape
    mp, dp = nx * CORES, nz * ny
    part = ff // nz
    sends = 2 * (2 * nz + nz * (nx - 1) + nz * nx + nz + nz * ny + 2 * nz * nx) * 2
    shapes = [(nz * rows, mp * feats)] * 2 + [(dp * depth, part), (part, dp * depth)]
    anywhere = pl.BlockSpec(memory_space=pl.ANY)
    return pl.pallas_call(
        functools.partial(gather_kernel, nz, ny, nx),
        out_shape=[jax.ShapeDtypeStruct(s, jnp.bfloat16) for s in shapes],
        in_specs=[anywhere] * 4,
        out_specs=[anywhere] * 4,
        scratch_shapes=[
            pltpu.SemaphoreType.DMA((sends,)),
            pltpu.SemaphoreType.DMA((2 * nz * mp,)),
            pltpu.SemaphoreType.DMA((2 * dp,)),
            pltpu.SemaphoreType.DMA((4,)),
        ],
        compiler_params=pltpu.CompilerParams(collective_id=0, has_side_effects=True),
        name="gather_all",
    )(tokens, grads, gate_weight, down_weight)


def sum_kernel(nz, ny, nx, part_ref, out_ref, slots, send, recv):
    d, m = lax.axis_index("dp"), lax.axis_index("mp")
    z, y = d // ny, d % ny
    mp = nx * CORES
    count = nz * mp
    me = z * mp + m

    def device(i):
        return (i // mp * ny + y, lax.rem(i, mp))

    barrier = pltpu.get_barrier_semaphore()
    for k in range(1, count):
        peer = device(lax.rem(me + k, count))
        pl.semaphore_signal(barrier, inc=1, device_id=peer, device_id_type=MESH)
    slots[me] = part_ref[...]
    pl.semaphore_wait(barrier, count - 1)

    def copy(k, to, into):
        return pltpu.make_async_remote_copy(
            src_ref=part_ref, dst_ref=slots.at[into], send_sem=send.at[k],
            recv_sem=recv.at[into], device_id=device(to), device_id_type=MESH,
        )

    for k in range(1, count):
        copy(k, lax.rem(me + k, count), me).start()
    for k in range(1, count):
        other = lax.rem(me + count - k, count)
        copy(k, other, other).wait_recv()
    total = slots[0]
    for i in range(1, count):
        total = total + slots[i]
    out_ref[...] = total
    for k in range(1, count):
        copy(k, lax.rem(me + k, count), me).wait_send()


def sum_over_parts(nz, ny, nx, tile):
    count = nz * nx * CORES
    vmem = pl.BlockSpec(memory_space=pltpu.VMEM)
    return pl.pallas_call(
        functools.partial(sum_kernel, nz, ny, nx),
        out_shape=jax.ShapeDtypeStruct(tile.shape, jnp.float32),
        in_specs=[vmem],
        out_specs=vmem,
        scratch_shapes=[
            pltpu.VMEM((count,) + tile.shape, jnp.float32),
            pltpu.SemaphoreType.DMA((count,)),
            pltpu.SemaphoreType.DMA((count,)),
        ],
        compiler_params=pltpu.CompilerParams(collective_id=1, has_side_effects=True),
        name="sum_over_parts",
    )(tile)


def shards(
    inputs, out_grads, gate_weight, down_weight, in_proj, out_proj, in_precond, out_precond,
    queries, languages,
):
    dp, mp = lax.axis_size("dp"), lax.axis_size("mp")
    nz, ny, nx = layout(dp, mp, gate_weight.shape[1])
    local_ex, seq_len, feats = inputs.shape
    rank = in_proj.shape[1]
    per_language = languages.shape[0] * dp // LANGS
    exact = lax.Precision.HIGHEST

    onehot = (languages[None, :] == jnp.arange(LANGS, dtype=jnp.int32)[:, None])
    lang_sum = jnp.dot(
        onehot.astype(jnp.bfloat16), queries, preferred_element_type=jnp.float32
    )
    lang_sum = lax.psum(lang_sum, "dp")
    m = lax.axis_index("mp")
    blocks = jnp.zeros((mp,) + lang_sum.shape, jnp.float32)
    for k in range(mp):
        ring = [(i, (i + k) % mp) for i in range(mp)]
        block = lax.ppermute(lang_sum, "mp", ring) if k else lang_sum
        blocks = lax.dynamic_update_index_in_dim(blocks, block, lax.rem(m + mp - k, mp), 0)
    lang_sum = blocks.swapaxes(0, 1).reshape(LANGS, rank, rank)
    turned = jnp.einsum("lij,bj->lib", lang_sum, out_precond, precision=exact)
    turned = jnp.einsum("ia,lib->lab", in_precond, turned, precision=exact)
    turned = turned / (seq_len * per_language)

    tok, grd, gate_all, down_all = gather_all(
        nz, ny, nx,
        inputs.reshape(local_ex * seq_len, feats),
        out_grads.reshape(local_ex * seq_len, feats),
        gate_weight, down_weight,
    )
    gate = jnp.dot(tok, gate_all, preferred_element_type=jnp.float32)
    hidden_grad = lax.dot_general(
        grd, down_all, (((1,), (1,)), ((), ())), preferred_element_type=jnp.float32
    )
    up_grad = (hidden_grad * jax.nn.silu(gate)).astype(jnp.bfloat16)
    part = gate_all.shape[1]
    d = lax.axis_index("dp")
    z = d // ny
    proj = lax.dynamic_slice_in_dim(out_proj, z * part, part, 0)
    out_part = jnp.dot(up_grad, proj, preferred_element_type=jnp.float32)
    in_part = jnp.dot(tok, in_proj, preferred_element_type=jnp.float32)
    cross = jnp.einsum(
        "esa,esb->eab",
        in_part.reshape(nz * local_ex, seq_len, rank),
        out_part.reshape(nz * local_ex, seq_len, rank),
        precision=exact,
    )
    partial = jnp.einsum("eab,lab->el", cross, turned, precision=exact)
    held = nz * local_ex
    tile = jnp.pad(partial, ((0, -held % 8), (0, -LANGS % 128)))
    total = sum_over_parts(nz, ny, nx, tile)[:, :LANGS]
    return lax.dynamic_slice_in_dim(total, z * local_ex, local_ex, 0)


def solution(mesh):
    return jax.shard_map(
        shards,
        mesh=mesh,
        in_specs=(
            P("dp", None, "mp"),
            P("dp", None, "mp"),
            P("dp", "mp"),
            P("mp", "dp"),
            P(),
            P("mp", None),
            P(),
            P(),
            P("dp", "mp"),
            P("dp"),
        ),
        out_specs=P("dp", None),
        check_vma=False,
    )
```
